256 devices in a mesh: dp: 32 (over x_hi, z, core), param: 8 (over y, x_lo).
Axes of the slice: x: 4 (x_hi: 2, x_lo: 2; x = x_hi * 2 + x_lo), y: 4, z: 8, core: 2. Of those that a mesh axis runs over, the one named last changes fastest.
Arguments:
- conv_input: bfloat16 [65536, 1024], P(('dp', 'param')), may hold values from -6 to 6
- block_dest: int32 [8192, 1], P(('dp', 'param')), may hold values from 0 to 31; in each aligned block of 32 rows (0 to 31, 32 to 63, ...) at most 2 rows name the same one
- live_frames: int32 [8192], P(('dp', 'param')), may hold values from 1 to 8
- conv_weight: bfloat16 [1024, 512], P('param'), may hold values from -0.1875 to 0.1875
- conv_gain: float32 [512], replicated, may hold values from 0.1 to 1.9
- conv_shift: float32 [512], replicated, may hold values from -3 to 3
- feat_gain: float32 [512], replicated, may hold values from 0.1 to 1.9
- feat_shift: float32 [512], replicated, may hold values from -3 to 3
- proj_weight: bfloat16 [512, 1920], P('param'), may hold values from -0.25 to 0.25
- proj_bias: float32 [1920], replicated, may hold values from -3 to 3
- cotangent: bfloat16 [131072, 1920], P(('dp', 'param')), may hold values from -6 to 6
Outputs:
- projected: float32 [131072, 1920], P(('dp', 'param'))
- frames_grad: float32 [65536, 1024], P(('dp', 'param'))
- conv_weight_grad: float32 [1024, 512], P('param')
- proj_weight_grad: float32 [512, 1920], P('param')
- norm_grads: float32 [4, 512], replicated
- bias_grad: float32 [1920], replicated
The draws below stay inside these ranges and needn't reach their ends.
Inputs may be any that keep to these rules, and one draw needn't show every extreme that they name: `block_dest`: each device sends at most 2 of its 32 segments to one index of dp, and some device sends exactly 2 to one.
All inputs are finite; a program needn't handle non-finite values.
Results may differ from the reference program's by a relative error of at most 0.003.
Values may be sent and summed in bfloat16 or wider, within the bound.
A program may use at most 64 MiB of HBM per device.

```python
import math
import jax
import jax.numpy as jnp
import numpy as np
from jax import lax

C = 512
D = 1920
BLK = 8
CAP = 2
NB = 32
W = 1024
FRAMES = 65536
BLOCKS = 8192
SLOTS = 512
OUT_ROWS = 131072
N_DP = 32
N_PARAM = 8


def touch_ends(entries, stream_key, smallest, high):
    longest = entries.shape.index(max(entries.shape))
    spots = []
    for shift in (0, 1):
        where = [jax.random.randint(jax.random.fold_in(stream_key, axis), (), 0, length) for axis, length in enumerate(entries.shape)]
        where[longest] = (where[longest] + shift) % entries.shape[longest]
        spots.append(tuple(where))
    return entries.at[spots[0]].set(smallest).at[spots[1]].set(high)


def block_levels(own_key, extent, cuts, least, high):
    factor_of = 1.0
    for axis_at, shards_of in cuts:
        draws = jax.random.uniform(jax.random.fold_in(jax.random.fold_in(own_key, 6), axis_at), (shards_of,), jnp.float32, least / len(cuts), high / len(cuts))
        factor_of = factor_of * jnp.repeat(jnp.exp(draws), extent[axis_at] // shards_of).reshape((-1,) + (1,) * (len(extent) - 1 - axis_at))
    return factor_of


def routed_block(stream_key, own, number, rows, number_of, top, reach, skew):
    ranking = jax.random.permutation(stream_key, number_of)
    heavy_load, ordinary = load_shares(number_of, rows * top, reach, skew, True), load_shares(number_of, rows * top, reach, skew, False)
    places = jnp.arange(number_of)

    def named(tallies, rotation):
        used = int((tallies > 0).sum())
        fixed = max(1, used // 4)
        shifted = fixed + (places - fixed + rotation * (used - fixed)) % max(1, number_of - fixed)
        return jnp.zeros((number_of,), jnp.int32).at[ranking[jnp.where(places < fixed, places, shifted)]].set(jnp.asarray(tallies, jnp.int32))

    tallies = jnp.where(number % 4 == 0, named(heavy_load, number // 4), named(ordinary, number - number // 4 - 1))
    mixed = jax.random.permutation(jax.random.fold_in(own, 3), number_of)
    donor, receiver = mixed[0:number_of // 2 * 2:2], mixed[1:number_of // 2 * 2:2]
    margin = jnp.minimum(tallies[donor] - 1, reach - tallies[receiver]) // 2
    margin = jnp.where((donor == ranking[0]) | (receiver == ranking[0]) | (tallies[receiver] == 0), 0, jnp.maximum(margin, 0))
    shifted = jax.random.randint(jax.random.fold_in(own, 4), (number_of // 2,), 0, 1 << 20) % (margin + 1)
    tallies = tallies.at[donor].add(-shifted).at[receiver].add(shifted)
    items = jnp.searchsorted(jnp.cumsum(tallies), jnp.arange(rows * top), side="right").astype(jnp.int32)
    table = items.reshape(top, rows).T
    table = table[jax.random.permutation(jax.random.fold_in(own, 1), rows)]
    rotation = jax.random.randint(jax.random.fold_in(own, 2), (rows, 1), 0, top)
    return jnp.take_along_axis(table, (jnp.arange(top)[None, :] + rotation) % top, axis=1)


def load_shares(amount, total, bound, slope, full):
    portions = [(1 << 20) // math.isqrt(standing ** slope) + 1 for standing in range(1, amount + 1)]
    largest = bound if full else min(bound, max(-(-total // amount), total * portions[0] // sum(portions)))
    least = 1 if total - largest >= amount - 1 else 0
    holding, surplus = [largest] + [least] * (amount - 1), total - largest - least * (amount - 1)
    while surplus > 0:
        candidates = [i for i in range(1, amount) if holding[i] < largest] or [i for i in range(1, amount) if holding[i] < bound]
        whole, left = sum([portions[i] for i in candidates]), surplus
        for i in candidates:
            addition = min(bound - holding[i], max(1, left * portions[i] // whole), surplus)
            holding[i] = holding[i] + addition
            surplus = surplus - addition
    return np.array(holding)


def scatter_about(own_key, shape, width, most, cuts=(), kind=jnp.bfloat16):
    values = width * jax.random.normal(own_key, shape, jnp.float32)
    if cuts:
        values = values * block_levels(own_key, shape, cuts, -0.22, 0.18)
    return jnp.clip(values, -most, most).astype(kind)


def setup_inputs(seed: int = 0) -> dict:
    streams_of = jax.random.split(jax.random.key(seed), 12)
    conv_input = scatter_about(streams_of[0], (FRAMES, W), 1.0, 6.0, ((0, 256),))
    block_dest_keys = jax.random.split(jax.random.fold_in(streams_of[1], 1), BLOCKS // NB)
    block_dest_turns = jax.random.permutation(jax.random.fold_in(streams_of[1], 3), BLOCKS // NB)
    block_dest = jax.vmap(lambda own, number: routed_block(jax.random.fold_in(streams_of[1], 2), own, number, NB, N_DP, 1, CAP, 2))(block_dest_keys, block_dest_turns).reshape((BLOCKS, 1))
    live_frames = touch_ends(jax.random.randint(streams_of[2], (BLOCKS,), 1, BLK + 1), jax.random.fold_in(streams_of[2], 1), 1, BLK).astype(jnp.int32)
    conv_weight = scatter_about(streams_of[3], (W, C), W ** -0.5, 0.1875, ((0, 8),))
    conv_gain = jnp.clip(1.0 + 0.18 * jax.random.normal(streams_of[4], (C,), jnp.float32), 0.1, 1.9)
    conv_shift = scatter_about(streams_of[5], (C,), 0.5, 3.0, (), jnp.float32)
    feat_gain = jnp.clip(1.0 + 0.18 * jax.random.normal(streams_of[6], (C,), jnp.float32), 0.1, 1.9)
    feat_shift = scatter_about(streams_of[7], (C,), 0.5, 3.0, (), jnp.float32)
    proj_weight = scatter_about(streams_of[8], (C, D), C ** -0.5, 0.25, ((0, 8),))
    proj_bias = scatter_about(streams_of[9], (D,), 0.5, 3.0, (), jnp.float32)
    cotangent = scatter_about(streams_of[10], (OUT_ROWS, D), 1.0, 6.0, ((0, 256),))
    return dict(conv_input=conv_input, block_dest=block_dest, live_frames=live_frames, conv_weight=conv_weight, conv_gain=conv_gain, conv_shift=conv_shift, feat_gain=feat_gain, feat_shift=feat_shift, proj_weight=proj_weight, proj_bias=proj_bias, cotangent=cotangent)


epsilon = 1e-05

def normalize(values, factor, offset):
    average = lax.optimization_barrier(jnp.mean(values, axis=-1, keepdims=True))
    centred = values - average
    spread = lax.optimization_barrier(jnp.mean(centred * centred, axis=-1, keepdims=True))
    return centred * lax.rsqrt(spread + epsilon) * factor + offset

def encode_tail(hidden, conv_gain, conv_shift, feat_gain, feat_shift):
    active = jax.nn.gelu(normalize(hidden, conv_gain, conv_shift), approximate=False)
    return normalize(active, feat_gain, feat_shift)

def contract_rows(left, right):
    return lax.dot_general(left, right, (((0,), (0,)), ((), ())), preferred_element_type=jnp.float32)

def contract_cols(left, right):
    return lax.dot_general(left, right, (((1,), (1,)), ((), ())), preferred_element_type=jnp.float32)

def reference(conv_input, block_dest, live_frames, conv_weight, conv_gain, conv_shift, feat_gain, feat_shift, proj_weight, proj_bias, cotangent):
    group_count = N_DP * N_PARAM
    grad_scale = 1.0 / math.sqrt(FRAMES)
    destination = block_dest.reshape(group_count, NB)
    onehot = (destination[:, :, None] == jnp.arange(N_DP, dtype=jnp.int32)[None, None, :]).astype(jnp.int32)
    earlier = jnp.cumsum(onehot, axis=1, dtype=jnp.int32) - onehot
    order_rank = lax.optimization_barrier(jnp.sum(earlier * onehot, axis=2, dtype=jnp.int32))
    group_index = jnp.arange(group_count, dtype=jnp.int32)[:, None]
    source_dp = group_index // N_PARAM
    source_param = group_index % N_PARAM
    first_row = (destination * N_PARAM + source_param) * SLOTS + (source_dp * CAP + order_rank) * BLK
    position = jnp.arange(BLK, dtype=jnp.int32)
    target = (first_row[:, :, None] + position[None, None, :]).reshape(FRAMES).astype(jnp.int32)
    live_mask = (position[None, :] < live_frames[:, None]).reshape(FRAMES)
    hidden = jnp.dot(conv_input, conv_weight, preferred_element_type=jnp.float32)
    tail_out, pullback = jax.vjp(encode_tail, hidden, conv_gain, conv_shift, feat_gain, feat_shift)
    features = tail_out.astype(jnp.bfloat16)
    lifted = jnp.dot(features, proj_weight, preferred_element_type=jnp.float32)
    outputs = jnp.where(live_mask[:, None], lifted + proj_bias, jnp.zeros((FRAMES, D), jnp.float32))
    projected = jnp.zeros((OUT_ROWS, D), jnp.float32).at[target].set(outputs)
    upstream = jnp.where(live_mask[:, None], cotangent[target], jnp.zeros((FRAMES, D), jnp.bfloat16))
    proj_weight_grad = contract_rows(features, upstream) * grad_scale
    bias_grad = lax.optimization_barrier(jnp.sum(upstream, axis=0, dtype=jnp.float32)) * grad_scale
    back_feat = contract_cols(upstream, proj_weight)
    grads = pullback(back_feat)
    hidden_back = grads[0].astype(jnp.bfloat16)
    norm_grads = jnp.stack([grads[1], grads[2], grads[3], grads[4]]) * grad_scale
    conv_weight_grad = contract_rows(conv_input, hidden_back) * grad_scale
    frames_grad = contract_cols(hidden_back, conv_weight)
    return (projected, frames_grad, conv_weight_grad, proj_weight_grad, norm_grads, bias_grad)
```

```python
import functools
import math

import jax
import jax.numpy as jnp
from jax import lax
from jax.experimental import pallas as pl
from jax.experimental.pallas import tpu as pltpu
from jax.sharding import PartitionSpec as P

CAP = 2
SEG = 8
MARK = 64.0
MESH = pl.DeviceIdType.MESH
VMEM = pltpu.VMEM

epsilon = 1e-05


def normalize(values, factor, offset):
    average = jnp.mean(values, axis=-1, keepdims=True)
    centred = values - average
    spread = jnp.mean(centred * centred, axis=-1, keepdims=True)
    return centred * lax.rsqrt(spread + epsilon) * factor + offset


def encode_tail(hidden, conv_gain, conv_shift, feat_gain, feat_shift):
    active = jax.nn.gelu(normalize(hidden, conv_gain, conv_shift), approximate=False)
    return normalize(active, feat_gain, feat_shift)


def contract_rows(left, right):
    return lax.dot_general(
        left, right, (((0,), (0,)), ((), ())), preferred_element_type=jnp.float32
    )


def contract_cols(left, right):
    return lax.dot_general(
        left, right, (((1,), (1,)), ((), ())), preferred_element_type=jnp.float32
    )


def remote(src, dst, send, recv, device):
    return pltpu.make_async_remote_copy(
        src_ref=src,
        dst_ref=dst,
        send_sem=send,
        recv_sem=recv,
        device_id=device,
        device_id_type=MESH,
    )


def loop(first, last, body):
    def step(index, carry):
        body(index)
        return carry

    lax.fori_loop(first, last, step, 0)


def greet(me_dp, me_par, n_dp, n_par):
    barrier = pltpu.get_barrier_semaphore()

    def over_dp(k):
        pl.semaphore_signal(
            barrier, inc=1, device_id=(lax.rem(me_dp + k, n_dp), me_par), device_id_type=MESH
        )

    def over_par(k):
        pl.semaphore_signal(
            barrier, inc=1, device_id=(me_dp, lax.rem(me_par + k, n_par)), device_id_type=MESH
        )

    loop(1, n_dp, over_dp)
    loop(1, n_par, over_par)
    pl.semaphore_wait(barrier, n_dp + n_par - 2)


def slot_targets(dest, live, frames, segments):
    seg = lax.broadcasted_iota(jnp.int32, (segments, frames), 0)
    frame = lax.broadcasted_iota(jnp.int32, (segments, frames), 1)
    owner = frame // SEG
    mine = owner == seg
    dest_all = jnp.broadcast_to(dest, (segments, frames)).astype(jnp.float32)
    live_all = jnp.broadcast_to(live, (segments, frames)).astype(jnp.float32)
    dest_row = jnp.sum(jnp.where(mine, dest_all, 0.0), axis=0, keepdims=True)
    live_row = jnp.sum(jnp.where(mine, live_all, 0.0), axis=0, keepdims=True)
    same = jnp.where(dest_all == dest_row, 1.0, 0.0)
    rank = jnp.sum(jnp.where(seg < owner, same, 0.0), axis=0, keepdims=True)
    position = (lax.broadcasted_iota(jnp.int32, (1, frames), 1) % SEG).astype(jnp.float32)
    row = (dest_row * CAP + rank) * SEG + position
    return jnp.where(position < live_row, row, -1.0)


def deliver_kernel(
    n_dp,
    n_par,
    conv_ref,
    dest_ref,
    live_ref,
    wc_ref,
    wp_ref,
    x_ref,
    wc_full,
    wp_full,
    place_ref,
    packed,
    x_send,
    x_recv,
    w_send,
    w_recv,
    f_send,
    f_recv,
):
    me_dp, me_par = lax.axis_index("dp"), lax.axis_index("param")
    core = lax.rem(me_dp, 2)
    mate = me_dp + 1 - 2 * core
    unit = CAP * SEG
    frames = conv_ref.shape[0]
    weights = ((wc_ref, wc_full), (wp_ref, wp_full))
    greet(me_dp, me_par, n_dp, n_par)

    def half_rows(ref, owner, which):
        rows = ref.shape[0]
        half = rows // 2
        return pl.ds(pl.multiple_of(owner * rows + which * half, half), half)

    def send_weight(w, k, shard, full):
        half = shard.shape[0] // 2
        return remote(
            shard.at[pl.ds(pl.multiple_of(core * half, half), half)],
            full.at[half_rows(shard, me_par, core)],
            w_send.at[w, k],
            w_recv.at[w, k],
            (me_dp, lax.rem(me_par + k, n_par)),
        )

    def pass_on(w, k, shard, full, which):
        rows = full.at[half_rows(shard, lax.rem(me_par + n_par - k, n_par), which)]
        return remote(rows, rows, f_send.at[w, k], f_recv.at[w, k], (mate, me_par))

    for w, (shard, full) in enumerate(weights):
        loop(1, n_par, lambda k: send_weight(w, k, shard, full).start())

    target = slot_targets(dest_ref[...], live_ref[...], frames, frames // SEG)
    block = 128

    def pack(t):
        rows = pl.ds(pl.multiple_of(t * block, block), block)
        here = (lax.broadcasted_iota(jnp.int32, (block, frames), 0) + t * block).astype(jnp.float32)
        hit = jnp.where(here == target, 1.0, 0.0)
        empty = 1.0 - jnp.sum(hit, axis=1, keepdims=True)
        place = hit.astype(jnp.bfloat16)
        place_ref[rows, :] = place
        moved = jnp.dot(place, conv_ref[...], preferred_element_type=jnp.float32)
        packed[rows, :] = (moved + empty * MARK).astype(jnp.bfloat16)

    loop(0, n_dp * unit // block, pack)

    def own_rows(index):
        return pl.ds(pl.multiple_of(index * unit, unit), unit)

    def send_rows(k):
        to = lax.rem(me_dp + k, n_dp)
        return remote(
            packed.at[own_rows(to)],
            x_ref.at[own_rows(me_dp)],
            x_send.at[k],
            x_recv.at[k],
            (to, me_par),
        )

    def recv_rows(k):
        source = lax.rem(me_dp + n_dp - k, n_dp)
        rows = x_ref.at[own_rows(source)]
        return remote(rows, rows, x_send.at[k], x_recv.at[k], (source, me_par))

    loop(1, n_dp, lambda k: send_rows(k).start())
    x_ref[own_rows(me_dp), :] = packed[own_rows(me_dp), :]
    for shard, full in weights:
        rows = shard.shape[0]
        full[pl.ds(pl.multiple_of(me_par * rows, rows), rows), :] = shard[...]

    for w, (shard, full) in enumerate(weights):

        def relay(k):
            rows = full.at[half_rows(shard, lax.rem(me_par + n_par - k, n_par), core)]
            remote(rows, rows, w_send.at[w, k], w_recv.at[w, k], (mate, me_par)).wait_recv()
            pass_on(w, k, shard, full, core).start()

        loop(1, n_par, relay)
    for w, (shard, full) in enumerate(weights):

        def settle(k):
            pass_on(w, k, shard, full, 1 - core).wait_recv()
            pass_on(w, k, shard, full, core).wait_send()
            send_weight(w, k, shard, full).wait_send()

        loop(1, n_par, settle)

    def finish(k):
        recv_rows(k).wait_recv()
        send_rows(k).wait_send()

    loop(1, n_dp, finish)


def deliver(conv_input, dest, live, conv_weight, proj_weight, n_dp, n_par):
    frames, width = conv_input.shape
    slots = n_dp * CAP * SEG
    whole = pl.BlockSpec(memory_space=VMEM)
    dma = pltpu.SemaphoreType.DMA
    return pl.pallas_call(
        functools.partial(deliver_kernel, n_dp, n_par),
        out_shape=(
            jax.ShapeDtypeStruct((slots, width), jnp.bfloat16),
            jax.ShapeDtypeStruct((conv_weight.shape[0] * n_par, conv_weight.shape[1]), jnp.bfloat16),
            jax.ShapeDtypeStruct((proj_weight.shape[0] * n_par, proj_weight.shape[1]), jnp.bfloat16),
            jax.ShapeDtypeStruct((slots, frames), jnp.bfloat16),
        ),
        in_specs=[whole] * 5,
        out_specs=(whole,) * 4,
        scratch_shapes=[
            pltpu.VMEM((slots, width), jnp.bfloat16),
            dma((n_dp,)),
            dma((n_dp,)),
            dma((2, n_par)),
            dma((2, n_par)),
            dma((2, n_par)),
            dma((2, n_par)),
        ],
        compiler_params=pltpu.CompilerParams(
            collective_id=0, has_side_effects=True, vmem_limit_bytes=32 * 1024 * 1024
        ),
        name="deliver",
    )(conv_input, dest, live, conv_weight, proj_weight)


def piece_grid(n_chip):
    side = math.isqrt(n_chip)
    return side, n_chip // side


def reduce_kernel(
    n_dp,
    n_par,
    scale,
    back_ref,
    gc_ref,
    gp_ref,
    gs_ref,
    ret_ref,
    oc_ref,
    op_ref,
    os_ref,
    c0c,
    c0p,
    s1c,
    s1p,
    r1c,
    r1p,
    r1s,
    s2c,
    s2p,
    s2s,
    r2c,
    r2p,
    r2s,
    b_send,
    b_recv,
    m_send,
    m_recv,
    p_send,
    p_recv,
    d_send,
    d_recv,
    e_send,
    e_recv,
    g_send,
    g_recv,
    h_send,
    h_recv,
    k_send,
    k_recv,
):
    me_dp, me_par = lax.axis_index("dp"), lax.axis_index("param")
    core = lax.rem(me_dp, 2)
    mate = me_dp + 1 - 2 * core
    n_chip = n_dp // 2
    me_chip = me_dp // 2
    unit = CAP * SEG
    greet(me_dp, me_par, n_dp, n_par)

    def own_rows(index):
        return pl.ds(pl.multiple_of(index * unit, unit), unit)

    def back_rows(k):
        to = lax.rem(me_dp + k, n_dp)
        return remote(
            back_ref.at[own_rows(to)],
            ret_ref.at[own_rows(me_dp)],
            b_send.at[k],
            b_recv.at[k],
            (to, me_par),
        )

    def back_wait(k):
        source = lax.rem(me_dp + n_dp - k, n_dp)
        rows = ret_ref.at[own_rows(source)]
        remote(rows, rows, b_send.at[k], b_recv.at[k], (source, me_par)).wait_recv()
        back_rows(k).wait_send()

    def par_at(k):
        return lax.rem(me_par + k, n_par)

    def from_par(k):
        return lax.rem(me_par + n_par - k, n_par)

    def halves(ref, which):
        half = ref.shape[1] // 2
        return pl.ds(pl.multiple_of(which * half, half), half)

    mates = ((gc_ref, c0c), (gp_ref, c0p))

    def to_mate(w, k):
        grad, landing = mates[w]
        block = par_at(k)
        return remote(
            grad.at[block, halves(grad, 1 - core)],
            landing.at[block],
            m_send.at[w, k],
            m_recv.at[w, k],
            (mate, me_par),
        )

    def start_mate(k):
        to_mate(0, k).start()
        to_mate(1, k).start()

    loop(1, n_par, start_mate)
    start_mate(0)

    def small_out(k):
        return remote(
            gs_ref.at[par_at(k)],
            r1s.at[k],
            p_send.at[2, k],
            p_recv.at[2, k],
            (me_dp, par_at(k)),
        )

    loop(1, n_par, lambda k: small_out(k).start())
    loop(1, n_dp, lambda k: back_rows(k).start())
    ret_ref[own_rows(me_dp), :] = back_ref[own_rows(me_dp), :]

    stages = ((s1c, r1c), (s1p, r1p))

    def to_par(w, k):
        sent, landing = stages[w]
        return remote(
            sent.at[k], landing.at[k], p_send.at[w, k], p_recv.at[w, k], (me_dp, par_at(k))
        )

    def summed(w, k):
        grad, landing = mates[w]
        to_mate(w, k).wait_recv()
        block = par_at(k)
        return grad[block, halves(grad, core), :] + landing[block]

    def pair_sum(k):
        for w in range(2):
            stages[w][0][k] = summed(w, k).astype(jnp.bfloat16)
            to_par(w, k).start()

    loop(1, n_par, pair_sum)
    s2c[...] = summed(0, 0)
    width = gp_ref.shape[2]
    s2p[:, width:] = jnp.zeros((s2p.shape[0], s2p.shape[1] - width), jnp.float32)
    s2p[:, :width] = summed(1, 0)
    s2s[...] = gs_ref[me_par]

    def gather_par(k):
        for w in range(2):
            to_par(w, k).wait_recv()
        small_out(k).wait_recv()
        s2c[...] += r1c[k].astype(jnp.float32)
        s2p[:, :width] += r1p[k].astype(jnp.float32)
        s2s[...] += r1s[k]

    loop(1, n_par, gather_par)

    rows_n, cols_n = piece_grid(n_chip)

    def region(shape, chip, top):
        tall, wide = shape[0] // rows_n, shape[1] // cols_n
        row, col = chip // cols_n, lax.rem(chip, cols_n)
        return (
            pl.ds(pl.multiple_of(top + row * tall, tall), tall),
            pl.ds(pl.multiple_of(col * wide, wide), wide),
        )

    def chip_at(k):
        return lax.rem(me_chip + k, n_chip)

    def chip_from(k):
        return lax.rem(me_chip + n_chip - k, n_chip)

    spread = ((s2c, r2c, oc_ref), (s2p, r2p, op_ref))

    def to_chip(w, k):
        held, landing, _ = spread[w]
        to = chip_at(k)
        return remote(
            held.at[region(held.shape, to, 0)],
            landing.at[k],
            d_send.at[w, k],
            d_recv.at[w, k],
            (to * 2 + core, me_par),
        )

    def start_chip(k):
        to_chip(0, k).start()
        to_chip(1, k).start()

    def small_dp(k):
        to = lax.rem(me_dp + k, n_dp)
        return remote(s2s, r2s.at[k], e_send.at[k], e_recv.at[k], (to, me_par))

    loop(1, n_chip, start_chip)
    loop(1, n_dp, lambda k: small_dp(k).start())

    def final_region(w, chip, which):
        held = spread[w][0]
        return region(held.shape, chip, which * held.shape[0])

    def from_chip(k):
        for w in range(2):
            to_chip(w, k).wait_recv()
            out = spread[w][2]
            out[final_region(w, me_chip, core)] += spread[w][1][k]

    for w in range(2):
        held, _, out = spread[w]
        out[final_region(w, me_chip, core)] = held[region(held.shape, me_chip, 0)]
    loop(1, n_chip, from_chip)
    for w in range(2):
        out = spread[w][2]
        out[final_region(w, me_chip, core)] = out[final_region(w, me_chip, core)] * scale

    def share(w, k):
        out = spread[w][2]
        rows = out.at[final_region(w, me_chip, core)]
        return remote(rows, rows, g_send.at[w, k], g_recv.at[w, k], (chip_at(k) * 2 + core, me_par))

    def share_wait(w, k):
        out = spread[w][2]
        rows = out.at[final_region(w, chip_from(k), core)]
        remote(
            rows, rows, g_send.at[w, k], g_recv.at[w, k], (chip_from(k) * 2 + core, me_par)
        ).wait_recv()

    def start_share(k):
        share(0, k).start()
        share(1, k).start()

    loop(1, n_chip, start_share)

    total = s2s[...]
    os_ref[me_par] = total

    def small_sum(k):
        small_dp(k).wait_recv()
        os_ref[me_par] += r2s[k]

    loop(1, n_dp, small_sum)
    os_ref[me_par] = os_ref[me_par] * scale

    def small_share(k, owner, to):
        rows = os_ref.at[owner]
        return remote(rows, rows, h_send.at[k], h_recv.at[k], (me_dp, to))

    loop(1, n_par, lambda k: small_share(k, me_par, par_at(k)).start())

    def end_share(k):
        share_wait(0, k)
        share_wait(1, k)

    loop(1, n_chip, end_share)

    def to_core(w, which):
        out = spread[w][2]
        half = out.shape[0] // 2
        rows = out.at[pl.ds(pl.multiple_of(which * half, half), half)]
        return remote(rows, rows, k_send.at[w], k_recv.at[w], (mate, me_par))

    for w in range(2):
        to_core(w, core).start()

    loop(1, n_dp, back_wait)

    def par_end(k):
        small_share(k, from_par(k), from_par(k)).wait_recv()
        small_share(k, me_par, par_at(k)).wait_send()
        small_out(k).wait_send()
        for w in range(2):
            to_par(w, k).wait_send()

    loop(1, n_par, par_end)

    def mate_end(k):
        for w in range(2):
            to_mate(w, k).wait_send()

    loop(0, n_par, mate_end)

    def chip_end(k):
        for w in range(2):
            to_chip(w, k).wait_send()
            share(w, k).wait_send()

    loop(1, n_chip, chip_end)
    loop(1, n_dp, lambda k: small_dp(k).wait_send())
    for w in range(2):
        to_core(w, 1 - core).wait_recv()
        to_core(w, core).wait_send()


def reduce_all(back, conv_grad, proj_grad, small, n_dp, n_par, scale):
    n_chip = n_dp // 2
    _, conv_rows, conv_cols = conv_grad.shape
    _, proj_rows, proj_cols = proj_grad.shape
    rows_n, cols_n = piece_grid(n_chip)
    wide = -(-proj_cols // (128 * cols_n)) * 128 * cols_n
    hc, hp = conv_rows // 2, proj_rows // 2
    tile = small.shape[1:]
    f32, b16 = jnp.float32, jnp.bfloat16
    whole = pl.BlockSpec(memory_space=VMEM)
    dma = pltpu.SemaphoreType.DMA
    return pl.pallas_call(
        functools.partial(reduce_kernel, n_dp, n_par, scale),
        out_shape=(
            jax.ShapeDtypeStruct(back.shape, b16),
            jax.ShapeDtypeStruct((conv_rows, conv_cols), f32),
            jax.ShapeDtypeStruct((proj_rows, wide), f32),
            jax.ShapeDtypeStruct(small.shape, f32),
        ),
        in_specs=[whole] * 4,
        out_specs=(whole,) * 4,
        scratch_shapes=[
            pltpu.VMEM((n_par, hc, conv_cols), f32),
            pltpu.VMEM((n_par, hp, proj_cols), f32),
            pltpu.VMEM((n_par, hc, conv_cols), b16),
            pltpu.VMEM((n_par, hp, proj_cols), b16),
            pltpu.VMEM((n_par, hc, conv_cols), b16),
            pltpu.VMEM((n_par, hp, proj_cols), b16),
            pltpu.VMEM((n_par,) + tile, f32),
            pltpu.VMEM((hc, conv_cols), f32),
            pltpu.VMEM((hp, wide), f32),
            pltpu.VMEM(tile, f32),
            pltpu.VMEM((n_chip, hc // rows_n, conv_cols // cols_n), f32),
            pltpu.VMEM((n_chip, hp // rows_n, wide // cols_n), f32),
            pltpu.VMEM((n_dp,) + tile, f32),
            dma((n_dp,)),
            dma((n_dp,)),
            dma((2, n_par)),
            dma((2, n_par)),
            dma((3, n_par)),
            dma((3, n_par)),
            dma((2, n_chip)),
            dma((2, n_chip)),
            dma((n_dp,)),
            dma((n_dp,)),
            dma((2, n_chip)),
            dma((2, n_chip)),
            dma((n_par,)),
            dma((n_par,)),
            dma((2,)),
            dma((2,)),
        ],
        compiler_params=pltpu.CompilerParams(
            collective_id=1, has_side_effects=True, vmem_limit_bytes=48 * 1024 * 1024
        ),
        name="reduce_all",
    )(back, conv_grad, proj_grad, small)


def on_device(
    conv_input,
    block_dest,
    live_frames,
    conv_weight,
    conv_gain,
    conv_shift,
    feat_gain,
    feat_shift,
    proj_weight,
    proj_bias,
    cotangent,
):
    n_dp = lax.axis_size("dp")
    n_par = lax.axis_size("param")
    frames_dev = conv_input.shape[0]
    grad_scale = 1.0 / math.sqrt(frames_dev * n_dp * n_par)
    arrived, conv_full, proj_full, place = deliver(
        conv_input, block_dest, live_frames[:, None], conv_weight, proj_weight, n_dp, n_par
    )
    live = arrived[:, :1] < MARK / 2
    rows = jnp.where(live, arrived, jnp.zeros_like(arrived))
    upstream = jnp.where(live, cotangent, jnp.zeros_like(cotangent))
    hidden = jnp.dot(rows, conv_full, preferred_element_type=jnp.float32)
    tail_out, pullback = jax.vjp(
        encode_tail, hidden, conv_gain, conv_shift, feat_gain, feat_shift
    )
    features = tail_out.astype(jnp.bfloat16)
    lifted = jnp.dot(features, proj_full, preferred_element_type=jnp.float32)
    projected = jnp.where(live, lifted + proj_bias, 0.0)
    proj_grad = contract_rows(features, upstream)
    back_feat = contract_cols(upstream, proj_full)
    grads = pullback(back_feat)
    hidden_back = grads[0].astype(jnp.bfloat16)
    conv_grad = contract_rows(rows, hidden_back)
    channels = conv_gain.shape[0]
    model = proj_bias.shape[0]
    bias_local = jnp.sum(upstream, axis=0, dtype=jnp.float32)
    small = jnp.concatenate([grads[1], grads[2], grads[3], grads[4], bias_local])
    small = jnp.pad(small, (0, n_par * 1024 - small.shape[0])).reshape(n_par, 8, 128)
    returned, conv_out, proj_out, small_out = reduce_all(
        hidden_back,
        conv_grad.reshape(n_par, -1, channels),
        proj_grad.reshape(n_par, -1, model),
        small,
        n_dp,
        n_par,
        grad_scale,
    )
    mine = contract_rows(place, returned).astype(jnp.bfloat16)
    frames_grad = contract_cols(mine, conv_full)
    flat = small_out.reshape(-1)
    return (
        projected,
        frames_grad,
        conv_out,
        proj_out[:, :model],
        flat[: 4 * channels].reshape(4, channels),
        flat[4 * channels : 4 * channels + model],
    )


def solution(mesh):
    return jax.shard_map(
        on_device,
        mesh=mesh,
        in_specs=(
            P(("dp", "param"), None),
            P(("dp", "param"), None),
            P(("dp", "param")),
            P("param", None),
            P(),
            P(),
            P(),
            P(),
            P("param", None),
            P(),
            P(("dp", "param"), None),
        ),
        out_specs=(
            P(("dp", "param"), None),
            P(("dp", "param"), None),
            P("param", None),
            P("param", None),
            P(),
            P(),
        ),
        check_vma=False,
    )
```

```python
import functools
import math

import jax
import jax.numpy as jnp
from jax import lax
from jax.experimental import pallas as pl
from jax.experimental.pallas import tpu as pltpu
from jax.sharding import PartitionSpec as P

CAP = 2
SEG = 8
UNIT = CAP * SEG
GROUP = 8
TILE = GROUP * UNIT
SUB = 32
MARK = 64.0
FIRST = 1152
KEEP = 32
MESH = pl.DeviceIdType.MESH

epsilon = 1e-05


def remote(src, dst, send, recv, device):
    return pltpu.make_async_remote_copy(
        src_ref=src,
        dst_ref=dst,
        send_sem=send,
        recv_sem=recv,
        device_id=device,
        device_id_type=MESH,
    )


def loop(first, last, body):
    def step(index, carry):
        body(index)
        return carry

    lax.fori_loop(first, last, step, 0)


def span(index, size):
    return pl.ds(pl.multiple_of(index * size, size), size)


def product(left, right, left_dim=1, right_dim=0):
    return lax.dot_general(
        left, right, (((left_dim,), (right_dim,)), ((), ())), preferred_element_type=jnp.float32
    )


def row_mean(values):
    return jnp.mean(values, axis=-1, keepdims=True)


def to_column(row):
    size = row.shape[1]
    down = lax.broadcasted_iota(jnp.int32, (size, size), 0)
    across = lax.broadcasted_iota(jnp.int32, (size, size), 1)
    spread = jnp.broadcast_to(row, (size, size))
    return jnp.sum(jnp.where(down == across, spread, 0.0), axis=1, keepdims=True)


def slot_targets(dest, live, frames):
    segments = frames // SEG
    seg = lax.broadcasted_iota(jnp.int32, (segments, frames), 0)
    frame = lax.broadcasted_iota(jnp.int32, (segments, frames), 1)
    owner = frame // SEG
    mine = owner == seg
    dest_all = jnp.broadcast_to(to_column(dest.astype(jnp.float32)), (segments, frames))
    live_all = jnp.broadcast_to(to_column(live.astype(jnp.float32)), (segments, frames))
    dest_row = jnp.sum(jnp.where(mine, dest_all, 0.0), axis=0, keepdims=True)
    live_row = jnp.sum(jnp.where(mine, live_all, 0.0), axis=0, keepdims=True)
    same = jnp.where(dest_all == dest_row, 1.0, 0.0)
    rank = jnp.sum(jnp.where(seg < owner, same, 0.0), axis=0, keepdims=True)
    position = (lax.broadcasted_iota(jnp.int32, (1, frames), 1) % SEG).astype(jnp.float32)
    row = (dest_row * CAP + rank) * SEG + position
    return jnp.where(position < live_row, row, -1.0)


def fold_rows(values):
    rows, cols = values.shape
    return jnp.sum(values.reshape(rows // 8, 8, cols), axis=0)


def tail_both(hidden, back, gain1, shift1, gain2, shift2):
    centred = hidden - row_mean(hidden)
    rate1 = lax.rsqrt(row_mean(centred * centred) + epsilon)
    norm1 = centred * rate1
    value = norm1 * gain1 + shift1
    cdf = 0.5 + 0.5 * lax.erf(value * (1.0 / math.sqrt(2.0)))
    active = value * cdf
    slope = cdf + value * (jnp.exp(value * value * -0.5) * (1.0 / math.sqrt(2.0 * math.pi)))
    centred2 = active - row_mean(active)
    rate2 = lax.rsqrt(row_mean(centred2 * centred2) + epsilon)
    norm2 = centred2 * rate2
    features = norm2 * gain2 + shift2
    d_norm2 = back * gain2
    back_active = rate2 * (d_norm2 - row_mean(d_norm2) - norm2 * row_mean(d_norm2 * norm2))
    back_value = back_active * slope
    d_norm1 = back_value * gain1
    back_hidden = rate1 * (d_norm1 - row_mean(d_norm1) - norm1 * row_mean(d_norm1 * norm1))
    return features, back_hidden, (back_value * norm1, back_value, back * norm2, back)

def exchange_kernel(
    n_dp,
    n_par,
    scale,
    conv_hbm,
    dest_ref,
    live_ref,
    wc_ref,
    wp_ref,
    cot_hbm,
    gain1_ref,
    shift1_ref,
    gain2_ref,
    shift2_ref,
    wc_hbm,
    wp_hbm,
    feat_hbm,
    mine_out,
    oc,
    op,
    osm,
    conv_in,
    cot,
    cot_m,
    wc_full,
    wp_full,
    packed,
    x_all,
    x_m,
    live_all,
    back_raw,
    hid,
    feat,
    feat_out,
    back_tile,
    ft,
    fm,
    lt,
    bt,
    bm,
    back,
    norm_acc,
    bias_row,
    gp1,
    gp2,
    gc1,
    gc2,
    r1p,
    r1c,
    r2p,
    r2c,
    t1p,
    t1c,
    t2p,
    t2c,
    u1p,
    u1c,
    u2p,
    u2c,
    sp,
    sc,
    cp,
    cc,
    small,
    small_m,
    sq,
    sr,
    ret,
    load_sem,
    store_sem,
    x_send,
    x_recv,
    w_send,
    w_recv,
    f_send,
    f_recv,
    b_send,
    b_recv,
    m_send,
    m_recv,
    a_send,
    a_recv,
    z_send,
    z_recv,
    s_send,
    s_recv,
    g_send,
    g_recv,
    k_send,
    k_recv,
):
    f32, b16 = jnp.float32, jnp.bfloat16
    me_dp, me_par = lax.axis_index("dp"), lax.axis_index("param")
    core = lax.rem(me_dp, 2)
    mate = me_dp + 1 - 2 * core
    me_chip = me_dp // 2
    n_chip = n_dp // 2
    n_z = n_chip // 2
    n_y = n_par // 2
    me_z = lax.rem(me_chip, n_z)
    x_hi = me_chip // n_z
    y, x_lo = me_par // 2, lax.rem(me_par, 2)
    x_me = x_lo * 2 + x_hi
    n_group = n_dp // GROUP
    me_group, me_in = me_dp // GROUP, lax.rem(me_dp, GROUP)
    frames = conv_in.shape[0]
    slots = x_all.shape[0]
    channels = gain1_ref.shape[1]
    model = cot.shape[1]

    def dp_at(k):
        return lax.rem(me_group + k // GROUP, n_group) * GROUP + lax.rem(
            me_in + lax.rem(k, GROUP), GROUP
        )

    def dp_from(k):
        return lax.rem(me_group - k // GROUP + n_group, n_group) * GROUP + lax.rem(
            me_in - lax.rem(k, GROUP) + GROUP, GROUP
        )

    def y_at(k):
        return lax.rem(y + k, n_y)

    def y_from(k):
        return lax.rem(y + n_y - k, n_y)

    def y_peer(k):
        return (me_dp, y_at(k) * 2 + x_lo)

    def x_at(k):
        low = 1 - x_lo if k & 2 else x_lo
        high = 1 - x_hi if k & 1 else x_hi
        return low, high

    def x_peer(k):
        low, high = x_at(k)
        return ((high * n_z + me_z) * 2 + core, y * 2 + low)

    def x_place(k):
        low, high = x_at(k)
        return low * 2 + high

    def z_peer(k):
        return ((x_hi * n_z + lax.rem(me_z + k, n_z)) * 2 + core, me_par)

    ours = (mate, me_par)

    shards = ((wc_ref, wc_full), (wp_ref, wp_full))
    loads = [
        pltpu.make_async_copy(conv_hbm, conv_in, load_sem.at[0]),
        pltpu.make_async_copy(cot_hbm, cot, load_sem.at[1]),
    ]
    for w, (shard, full) in enumerate(shards):
        rows = full.at[span(me_par, shard.shape[0])]
        loads.append(pltpu.make_async_copy(shard, rows, load_sem.at[2 + w]))
    for load in loads:
        load.start()
    barrier = pltpu.get_barrier_semaphore()

    def greet(device):
        pl.semaphore_signal(barrier, inc=1, device_id=device, device_id_type=MESH)

    loop(1, n_dp, lambda k: greet((dp_at(k), me_par)))
    loop(1, n_y, lambda k: greet(y_peer(k)))
    greet(x_peer(2))
    greet(x_peer(3))

    target = slot_targets(dest_ref[...], live_ref[...], frames)
    loads[0].wait()

    def pack(t):
        rows = span(t, TILE)
        here = (lax.broadcasted_iota(jnp.int32, (TILE, frames), 0) + t * TILE).astype(f32)
        hit = jnp.where(here == target, 1.0, 0.0)
        empty = 1.0 - jnp.sum(hit, axis=1, keepdims=True)
        moved = product(hit.astype(b16), conv_in[...])
        packed[rows, :] = (moved + empty * MARK).astype(b16)

    loop(0, slots // TILE, pack)
    pl.semaphore_wait(barrier, n_dp + n_y)

    own_steps = [1] + [2 * k for k in range(1, n_y)]
    far_steps = [2 * k + 1 for k in range(1, n_y)]

    def weight_rows(w, s, which):
        shard, full = shards[w]
        flip = lax.rem(s, 2)
        low = x_lo + flip - 2 * flip * x_lo
        owner = y_from(s // 2) * 2 + low
        return full.at[span(owner * 2 + which, shard.shape[0] // 2)]

    def send_weight(w, s):
        shard, full = shards[w]
        half = shard.shape[0] // 2
        low = 1 - x_lo if s in far_steps else x_lo
        place = full.at[span((y * 2 + low) * 2 + core, half)]
        source = place if s in far_steps else shard.at[span(core, half)]
        device = x_peer(2) if s == 1 else y_peer(s // 2)
        return remote(source, place, w_send.at[w, s], w_recv.at[w, s], device)

    def await_weight(w, s):
        rows = weight_rows(w, s, core)
        remote(rows, rows, w_send.at[w, s], w_recv.at[w, s], ours).wait_recv()

    def pass_on(w, s, which):
        rows = weight_rows(w, s, which)
        return remote(rows, rows, f_send.at[w, s], f_recv.at[w, s], ours)

    def send_rows(k):
        to = dp_at(k)
        return remote(
            packed.at[span(to, UNIT)],
            x_all.at[span(me_dp, UNIT)],
            x_send.at[k],
            x_recv.at[k],
            (to, me_par),
        )

    def recv_rows(k):
        source = dp_from(k)
        rows = x_all.at[span(source, UNIT)]
        return remote(rows, rows, x_send.at[k], x_recv.at[k], (source, me_par))

    for w in range(2):
        for s in own_steps:
            send_weight(w, s).start()
    loop(1, n_dp, lambda k: send_rows(k).start())
    cot_share = remote(cot_hbm, cot_m, k_send.at[0], k_recv.at[0], ours)
    cot_share.start()
    x_all[span(me_dp, UNIT), :] = packed[span(me_dp, UNIT), :]
    for w in range(2):
        await_weight(w, 1)
        for s in far_steps:
            send_weight(w, s).start()
        pass_on(w, 1, core).start()
    for w in range(2):

        def relay(s):
            await_weight(w, s)
            pass_on(w, s, core).start()

        loop(2, 2 * n_y, relay)
    for w in range(2):
        loop(1, 2 * n_y, lambda s: pass_on(w, s, 1 - core).wait_recv())
    for load in loads[1:]:
        load.wait()
    keep_weights = [
        pltpu.make_async_copy(wc_full, wc_hbm, store_sem.at[n_group]),
        pltpu.make_async_copy(wp_full, wp_hbm, store_sem.at[n_group + 1]),
    ]
    for copy in keep_weights:
        copy.start()

    def back_product(t):
        rows = span(t, TILE)
        back_raw[rows, :] = product(cot[rows, :], wp_full[...], 1, 1)

    loop(0, slots // TILE, back_product)
    norm_acc[...] = jnp.zeros_like(norm_acc)

    def tile_rows(t):
        return span(lax.rem(me_group - t + n_group, n_group), TILE)

    def store_rows(t):
        rows = tile_rows(t)
        return pltpu.make_async_copy(feat_out.at[rows], feat_hbm.at[rows], store_sem.at[t])

    def mate_x(t):
        rows = tile_rows(t)
        return remote(x_all.at[rows], x_m.at[rows], m_send.at[0, t], m_recv.at[0, t], ours)

    def mate_feat(t):
        cols = tile_rows(t)
        return remote(
            ft.at[:, 1 - core, :, cols], fm.at[:, :, cols], m_send.at[1, t], m_recv.at[1, t], ours
        )

    def mate_back(t):
        cols = tile_rows(t)
        return remote(
            bt.at[1 - core, :, cols], bm.at[:, cols], m_send.at[2, t], m_recv.at[2, t], ours
        )

    def tile(t):
        group = lax.rem(me_group - t + n_group, n_group)
        rows = tile_rows(t)
        loop(jnp.maximum(1, t * GROUP), (t + 1) * GROUP, lambda k: recv_rows(k).wait_recv())
        arrived = x_all[rows, :]
        live = jnp.where(arrived[:, :1].astype(f32) < MARK / 2, 1.0, 0.0)
        live_all[rows, :] = jnp.broadcast_to(live, (TILE, 128))
        kept = arrived * live.astype(b16)
        x_all[rows, :] = kept
        mate_x(t).start()
        hid[...] = product(kept, wc_full[...])

        def few(u):
            sub = span(u, SUB)
            here = pl.ds(pl.multiple_of(group * TILE + u * SUB, SUB), SUB)
            keep = live_all[here, :][:, :1]
            features, grad, terms = tail_both(
                hid[sub, :],
                back_raw[here, :] * keep,
                gain1_ref[...],
                shift1_ref[...],
                gain2_ref[...],
                shift2_ref[...],
            )
            feat[sub, :] = features * keep
            back_tile[sub, :] = grad
            for n, term in enumerate(terms):
                norm_acc[n] += fold_rows(term)

        loop(0, TILE // SUB, few)
        ft[:, :, :, rows] = feat[...].T.astype(b16).reshape(ft.shape[:3] + (TILE,))
        mate_feat(t).start()
        bt[:, :, rows] = back_tile[...].T.astype(b16).reshape(bt.shape[:2] + (TILE,))
        mate_back(t).start()
        lt[:, rows] = live_all[rows, :].T[: lt.shape[0]].astype(b16)
        back[rows, :] = back_tile[...].astype(b16)
        feat_out[rows, :channels] = feat[...].astype(b16)
        feat_out[rows, channels:] = live_all[rows, :].astype(b16)
        store_rows(t).start()

    loop(0, n_group, tile)

    half = channels // 2
    loop(0, n_group, lambda t: mate_feat(t).wait_recv())
    cot_share.wait_recv()
    step = 384

    def proj_part(cols):
        left = jnp.concatenate([ft[:, core].reshape(half, slots), lt[...]], axis=0)
        own = product(left, cot[:, cols])
        bias_row[:, cols] = own[half : half + 1]
        both = own[:half] + product(fm[...].reshape(half, slots), cot_m[:, cols])
        return both.astype(b16).reshape(n_y, 4, half // n_par // 2, step)

    def proj_first(n):
        gp1[:, :, :, span(n, step)] = proj_part(span(n, step))

    def proj_second(n):
        gp2[:, :, :, span(n, step)] = proj_part(
            pl.ds(pl.multiple_of(n * step + FIRST, 128), step)
        )

    def first_y(k, w):
        held, landing = ((gp1, r1p), (gc1, r1c))[w]
        return remote(
            held.at[y_at(k)], landing.at[k], a_send.at[w, k], a_recv.at[w, k], y_peer(k)
        )

    def second_x(k, w):
        held, landing = ((gp2, r2p), (gc2, r2c))[w]
        return remote(
            held.at[:, x_place(k)],
            landing.at[k],
            a_send.at[2 + w, k],
            a_recv.at[2 + w, k],
            x_peer(k),
        )

    offsets = range(1, 4)
    loop(0, FIRST // step, proj_first)
    for k in offsets:
        first_y(k, 0).start()
    loop(0, (model - FIRST) // step, proj_second)
    for k in offsets:
        second_x(k, 0).start()

    loop(0, n_group, lambda t: mate_back(t).wait_recv())
    loop(0, n_group, lambda t: mate_x(t).wait_recv())
    width = oc.shape[1]
    rest = half // 2 - KEEP

    def conv_part(n):
        cols = span(n, 2 * width)
        pair = product(bt[core], x_all[:, cols]) + product(bm[...], x_m[:, cols])
        pair = pair.astype(b16)
        for low in range(2):
            block = pair[:, low * width : (low + 1) * width]
            for high in range(2):
                top = high * (half // 2)
                gc1[n, low * 2 + high] = block[top : top + KEEP]
                gc2[n, low * 2 + high] = block[top + KEEP : top + KEEP + rest]

    loop(0, n_y, conv_part)
    for k in offsets:
        first_y(k, 1).start()
    for k in offsets:
        second_x(k, 1).start()

    lanes = 128
    per = channels // lanes
    small[...] = jnp.zeros_like(small)
    for v in range(4):
        total = jnp.sum(norm_acc[v], axis=0, keepdims=True)
        for q in range(per):
            at = per * v + q
            small[at : at + 1, :] = total[:, q * lanes : (q + 1) * lanes]
    for q in range(model // lanes):
        at = per * 4 + q
        small[at : at + 1, :] = bias_row[:, q * lanes : (q + 1) * lanes]
    share_small = remote(small, small_m, k_send.at[1], k_recv.at[1], ours)
    share_small.start()

    def back_rows(k):
        to = dp_at(k)
        return remote(
            back.at[span(to, UNIT)],
            ret.at[span(me_dp, UNIT)],
            b_send.at[k],
            b_recv.at[k],
            (to, me_par),
        )

    def back_wait(k):
        source = dp_from(k)
        rows = ret.at[span(source, UNIT)]
        remote(rows, rows, b_send.at[k], b_recv.at[k], (source, me_par)).wait_recv()

    loop(1, n_dp, lambda k: back_rows(k).start())
    ret[span(me_dp, UNIT), :] = back[span(me_dp, UNIT), :]

    few_rows = small.shape[0] // 2

    def small_step(stage, k):
        device = (y_peer, x_peer, z_peer)[stage](k)
        return remote(
            sq.at[stage], sr.at[stage, k], s_send.at[stage, k], s_recv.at[stage, k], device
        )

    def small_sum(stage, count):
        total = sq[stage]
        for k in range(1, count):
            small_step(stage, k).wait_recv()
            total = total + sr[stage, k]
        return total

    share_small.wait_recv()
    sq[0] = small[span(core, few_rows), :] + small_m[span(core, few_rows), :]
    for k in offsets:
        small_step(0, k).start()

    def then_x(k, w):
        held, landing = ((t1p, u1p), (t1c, u1c))[w]
        return remote(
            held.at[x_place(k)], landing.at[k], a_send.at[4 + w, k], a_recv.at[4 + w, k], x_peer(k)
        )

    def then_y(k, w):
        held, landing = ((t2p, u2p), (t2c, u2c))[w]
        return remote(
            held.at[y_at(k)], landing.at[k], a_send.at[6 + w, k], a_recv.at[6 + w, k], y_peer(k)
        )

    for k in offsets:
        first_y(k, 0).wait_recv()
    total = gp1[y].astype(f32)
    for k in offsets:
        total = total + r1p[k].astype(f32)
    t1p[...] = total
    for k in offsets:
        then_x(k, 0).start()
    for k in offsets:
        second_x(k, 0).wait_recv()
    total = gp2[:, x_me].astype(f32)
    for k in offsets:
        total = total + r2p[k].astype(f32)
    t2p[...] = total
    for k in offsets:
        then_y(k, 0).start()
    for k in offsets:
        first_y(k, 1).wait_recv()
    total = gc1[y].astype(f32)
    for k in offsets:
        total = total + r1c[k].astype(f32)
    t1c[...] = total
    for k in offsets:
        then_x(k, 1).start()
    for k in offsets:
        second_x(k, 1).wait_recv()
    total = gc2[:, x_me].astype(f32)
    for k in offsets:
        total = total + r2c[k].astype(f32)
    t2c[...] = total
    for k in offsets:
        then_y(k, 1).start()
    sq[1] = small_sum(0, 4)
    for k in offsets:
        small_step(1, k).start()

    sp[:, model:] = jnp.zeros((sp.shape[0], sp.shape[1] - model), f32)
    for k in offsets:
        then_x(k, 0).wait_recv()
    sp[:, :FIRST] = t1p[x_me] + u1p[1] + u1p[2] + u1p[3]
    for k in offsets:
        then_y(k, 0).wait_recv()
    sp[:, FIRST:model] = t2p[y] + u2p[1] + u2p[2] + u2p[3]
    for k in offsets:
        then_x(k, 1).wait_recv()
    sc[:KEEP, :] = t1c[x_me] + u1c[1] + u1c[2] + u1c[3]
    for k in offsets:
        then_y(k, 1).wait_recv()
    sc[KEEP:, :] = t2c[y] + u2c[1] + u2c[2] + u2c[3]

    wide = sp.shape[1] // n_z
    tall = sc.shape[0] // n_z

    def over_z(k, w):
        to = lax.rem(me_z + k, n_z)
        held = sp.at[:, span(to, wide)] if w == 0 else sc.at[span(to, tall)]
        landing = cp if w == 0 else cc
        return remote(held, landing.at[k], z_send.at[w, k], z_recv.at[w, k], z_peer(k))

    def start_z(k):
        over_z(k, 0).start()
        over_z(k, 1).start()

    loop(1, n_z, start_z)
    sq[2] = small_sum(1, 4)
    for k in range(1, n_z):
        small_step(2, k).start()

    def proj_place(chip):
        return (
            span(core * 2 + chip // n_z, sp.shape[0]),
            span(lax.rem(chip, n_z), wide),
        )

    def conv_place(chip):
        return span(core * n_chip + chip, tall)

    def wait_z(k):
        over_z(k, 0).wait_recv()
        over_z(k, 1).wait_recv()

    loop(1, n_z, wait_z)
    total = sp[:, span(me_z, wide)]
    for k in range(1, n_z):
        total = total + cp[k]
    op[proj_place(me_chip)] = total * scale
    total = sc[span(me_z, tall), :]
    for k in range(1, n_z):
        total = total + cc[k]
    oc[conv_place(me_chip), :] = total * scale

    def chip_at(k):
        return lax.rem(me_chip + k, n_chip)

    def chip_from(k):
        return lax.rem(me_chip + n_chip - k, n_chip)

    def share(w, k, chip, other):
        rows = op.at[proj_place(chip)] if w == 0 else oc.at[conv_place(chip)]
        return remote(rows, rows, g_send.at[w, k], g_recv.at[w, k], (other * 2 + core, me_par))

    def start_share(k):
        share(0, k, me_chip, chip_at(k)).start()
        share(1, k, me_chip, chip_at(k)).start()

    loop(1, n_chip, start_share)
    osm[span(core, few_rows), :] = small_sum(2, n_z) * scale

    def to_core(w, which):
        held = (op, oc, osm)[w]
        rows = held.at[span(which, held.shape[0] // 2)]
        return remote(rows, rows, k_send.at[2 + w], k_recv.at[2 + w], ours)

    to_core(2, core).start()

    loop(1, n_dp, back_wait)
    column = to_column(target)
    part = frames // 2
    for h in range(2):
        slot = lax.broadcasted_iota(jnp.int32, (part, slots), 1).astype(f32)
        pick = jnp.where(slot == column[h * part : (h + 1) * part], 1.0, 0.0).astype(b16)
        mine_out[h * part : (h + 1) * part, :] = product(pick, ret[...]).astype(b16)

    def weight_end(s):
        for w in range(2):
            pass_on(w, s, core).wait_send()

    loop(1, 2 * n_y, weight_end)
    for w in range(2):
        for s in own_steps + far_steps:
            send_weight(w, s).wait_send()
    for k in offsets:
        for w in range(2):
            first_y(k, w).wait_send()
            second_x(k, w).wait_send()
            then_x(k, w).wait_send()
            then_y(k, w).wait_send()
    for stage, count in ((0, 4), (1, 4), (2, n_z)):
        for k in range(1, count):
            small_step(stage, k).wait_send()

    def tile_end(t):
        mate_x(t).wait_send()
        mate_feat(t).wait_send()
        mate_back(t).wait_send()
        store_rows(t).wait()

    loop(0, n_group, tile_end)
    for copy in keep_weights:
        copy.wait()
    cot_share.wait_send()
    share_small.wait_send()

    def z_end(k):
        over_z(k, 0).wait_send()
        over_z(k, 1).wait_send()

    loop(1, n_z, z_end)

    def dp_end(k):
        send_rows(k).wait_send()
        back_rows(k).wait_send()

    loop(1, n_dp, dp_end)

    def end_share(k):
        share(0, k, chip_from(k), chip_from(k)).wait_recv()
        share(1, k, chip_from(k), chip_from(k)).wait_recv()

    loop(1, n_chip, end_share)
    to_core(0, core).start()
    to_core(1, core).start()

    def chip_end(k):
        for w in range(2):
            share(w, k, me_chip, chip_at(k)).wait_send()

    loop(1, n_chip, chip_end)
    for w in range(3):
        to_core(w, 1 - core).wait_recv()
        to_core(w, core).wait_send()


def finish_kernel(
    feat_ref,
    wp_ref,
    bias_ref,
    mine_ref,
    wc_ref,
    oc_ref,
    op_ref,
    osm_ref,
    projected_ref,
    frames_ref,
    conv_out,
    proj_out,
    norm_out,
    bias_out,
):
    channels = wp_ref.shape[0]
    model = wp_ref.shape[1]
    live = feat_ref[:, channels : channels + 1].astype(jnp.float32)
    lifted = product(feat_ref[:, :channels], wp_ref[...]) + bias_ref[...].reshape(1, model)
    projected_ref[...] = lifted * live
    frames_ref[...] = product(mine_ref[...], wc_ref[...], 1, 1)

    @pl.when(pl.program_id(0) == 0)
    def _():
        lanes = osm_ref.shape[1]
        per = channels // lanes
        conv_out[...] = oc_ref[...].T
        proj_out[...] = op_ref[:, :model]
        for v in range(4):
            for q in range(per):
                at = per * v + q
                norm_out[v : v + 1, q * lanes : (q + 1) * lanes] = osm_ref[at : at + 1, :]
        for q in range(model // lanes):
            bias_out[q * lanes : (q + 1) * lanes] = osm_ref[4 * per + q, :]


def on_device(
    conv_input,
    block_dest,
    live_frames,
    conv_weight,
    conv_gain,
    conv_shift,
    feat_gain,
    feat_shift,
    proj_weight,
    proj_bias,
    cotangent,
):
    n_dp = lax.axis_size("dp")
    n_par = lax.axis_size("param")
    n_chip = n_dp // 2
    n_z = n_chip // 2
    n_y = n_par // 2
    n_group = n_dp // GROUP
    frames, width = conv_input.shape
    slots = n_dp * UNIT
    channels = conv_gain.shape[0]
    model = proj_bias.shape[0]
    conv_rows, proj_rows = conv_weight.shape[0], proj_weight.shape[0]
    padded = -(-model // (128 * n_z)) * 128 * n_z
    hp = proj_rows // 4
    hc = channels // 4
    second = model - FIRST
    scale = 1.0 / math.sqrt(frames * n_dp * n_par)
    f32, b16 = jnp.float32, jnp.bfloat16
    vmem = pl.BlockSpec(memory_space=pltpu.VMEM)
    hbm = pl.BlockSpec(memory_space=pl.ANY)
    dma = pltpu.SemaphoreType.DMA
    buf = pltpu.VMEM
    out = jax.ShapeDtypeStruct
    wc_full, wp_full, feat, mine, oc, op, osm = pl.pallas_call(
        functools.partial(exchange_kernel, n_dp, n_par, scale),
        out_shape=(
            out((width, channels), b16),
            out((channels, model), b16),
            out((slots, channels + 128), b16),
            out((frames, channels), b16),
            out((channels, conv_rows), f32),
            out((proj_rows, padded), f32),
            out((32, 128), f32),
        ),
        in_specs=[hbm, vmem, vmem, hbm, hbm, hbm, vmem, vmem, vmem, vmem],
        out_specs=(hbm, hbm, hbm, vmem, vmem, vmem, vmem),
        scratch_shapes=[
            buf((frames, width), b16),
            buf((slots, model), b16),
            buf((slots, model), b16),
            buf((width, channels), b16),
            buf((channels, model), b16),
            buf((slots, width), b16),
            buf((slots, width), b16),
            buf((slots, width), b16),
            buf((slots, 128), f32),
            buf((slots, channels), f32),
            buf((TILE, channels), f32),
            buf((TILE, channels), f32),
            buf((slots, channels + 128), b16),
            buf((TILE, channels), f32),
            buf((n_par, 2, proj_rows // 2, slots), b16),
            buf((n_par, proj_rows // 2, slots), b16),
            buf((16, slots), b16),
            buf((2, channels // 2, slots), b16),
            buf((channels // 2, slots), b16),
            buf((slots, channels), b16),
            buf((4, 8, channels), f32),
            buf((1, model), f32),
            buf((n_y, 4, hp, FIRST), b16),
            buf((n_y, 4, hp, second), b16),
            buf((n_y, 4, KEEP, conv_rows), b16),
            buf((n_y, 4, hc - KEEP, conv_rows), b16),
            buf((4, 4, hp, FIRST), b16),
            buf((4, 4, KEEP, conv_rows), b16),
            buf((4, n_y, hp, second), b16),
            buf((4, n_y, hc - KEEP, conv_rows), b16),
            buf((4, hp, FIRST), f32),
            buf((4, KEEP, conv_rows), f32),
            buf((n_y, hp, second), f32),
            buf((n_y, hc - KEEP, conv_rows), f32),
            buf((4, hp, FIRST), f32),
            buf((4, KEEP, conv_rows), f32),
            buf((4, hp, second), f32),
            buf((4, hc - KEEP, conv_rows), f32),
            buf((hp, padded), f32),
            buf((hc, conv_rows), f32),
            buf((n_z, hp, padded // n_z), f32),
            buf((n_z, hc // n_z, conv_rows), f32),
            buf((32, 128), f32),
            buf((32, 128), f32),
            buf((3, 16, 128), f32),
            buf((3, n_z, 16, 128), f32),
            buf((slots, channels), b16),
            dma((4,)),
            dma((n_group + 2,)),
            dma((n_dp,)),
            dma((n_dp,)),
            dma((2, n_par)),
            dma((2, n_par)),
            dma((2, n_par)),
            dma((2, n_par)),
            dma((n_dp,)),
            dma((n_dp,)),
            dma((3, n_group)),
            dma((3, n_group)),
            dma((8, 4)),
            dma((8, 4)),
            dma((2, n_z)),
            dma((2, n_z)),
            dma((3, n_z)),
            dma((3, n_z)),
            dma((2, n_chip)),
            dma((2, n_chip)),
            dma((5,)),
            dma((5,)),
        ],
        compiler_params=pltpu.CompilerParams(
            collective_id=0, has_side_effects=True, vmem_limit_bytes=56 * 1024 * 1024
        ),
        name="exchange",
    )(
        conv_input,
        block_dest.reshape(1, -1),
        live_frames.reshape(1, -1),
        conv_weight,
        proj_weight,
        cotangent,
        conv_gain.reshape(1, -1),
        conv_shift.reshape(1, -1),
        feat_gain.reshape(1, -1),
        feat_shift.reshape(1, -1),
    )
    steps = 4

    def fixed(array):
        return pl.BlockSpec(array.shape, lambda i: (0,) * array.ndim)

    def rows_of(count, cols):
        return pl.BlockSpec((count // steps, cols), lambda i: (i, 0))

    outs = (
        out((slots, model), f32),
        out((frames, width), f32),
        out((conv_rows, channels), f32),
        out((proj_rows, model), f32),
        out((4, channels), f32),
        out((model,), f32),
    )
    return pl.pallas_call(
        finish_kernel,
        grid=(steps,),
        out_shape=outs,
        in_specs=[
            rows_of(slots, channels + 128),
            fixed(wp_full),
            fixed(proj_bias),
            rows_of(frames, channels),
            fixed(wc_full),
            fixed(oc),
            fixed(op),
            fixed(osm),
        ],
        out_specs=(rows_of(slots, model), rows_of(frames, width)) + tuple(fixed(o) for o in outs[2:]),
        compiler_params=pltpu.CompilerParams(vmem_limit_bytes=56 * 1024 * 1024),
        name="finish",
    )(feat, wp_full, proj_bias, mine, wc_full, oc, op, osm)


def solution(mesh):
    return jax.shard_map(
        on_device,
        mesh=mesh,
        in_specs=(
            P(("dp", "param"), None),
            P(("dp", "param"), None),
            P(("dp", "param")),
            P("param", None),
            P(),
            P(),
            P(),
            P(),
            P("param", None),
            P(),
            P(("dp", "param"), None),
        ),
        out_specs=(
            P(("dp", "param"), None),
            P(("dp", "param"), None),
            P("param", None),
            P("param", None),
            P(),
            P(),
        ),
        check_vma=False,
    )
```
